256 devices in a mesh: grp: 4 (over y), shard: 64 (over z, x, core).
Axes of the slice: x: 4, y: 4, z: 8, core: 2. Of those that a mesh axis runs over, the one named last changes fastest.
Arguments:
- head_vecs: bfloat16 [131072, 512], P(('grp', 'shard')), may hold values from -2 to 2
- tail_vecs: bfloat16 [131072, 512], P(('grp', 'shard')), may hold values from -2 to 2
- rel_id: int32 [131072], P(('grp', 'shard')), may hold values from 0 to 3
- head_owner: int32 [131072, 1], P(('grp', 'shard')), may hold values from 0 to 63; in each aligned block of 512 rows (0 to 511, 512 to 1023, ...) at most 16 rows name the same one
- head_row: int32 [131072], P(('grp', 'shard')), may hold values from 0 to 2047
- tail_owner: int32 [131072, 1], P(('grp', 'shard')), may hold values from 0 to 63; in each aligned block of 512 rows (0 to 511, 512 to 1023, ...) at most 16 rows name the same one
- tail_row: int32 [131072], P(('grp', 'shard')), may hold values from 0 to 2047
- neg_vecs: bfloat16 [4096, 512], P(('grp', 'shard')), may hold values from -2 to 2
- neg_owner: int32 [4096, 1], P(('grp', 'shard')), may hold values from 0 to 63; in each aligned block of 16 rows (0 to 15, 16 to 31, ...) at most 2 rows name the same one
- neg_row: int32 [4096], P(('grp', 'shard')), may hold values from 0 to 2047
- counts: int32 [4, 64], P('grp', 'shard'), may hold values from 1 to 512, 20480 in all within a row
- relations: bfloat16 [4, 512, 512], replicated, may hold values from -0.1 to 1.1
Outputs:
- entity_grad: float32 [4, 131072, 512], P('grp', 'shard')
- relation_grad: float32 [2048, 512], P(('grp', 'shard'))
The draws below stay inside these ranges and needn't reach their ends.
Inputs may be any that keep to these rules, and one draw needn't show every extreme that they name: `head_owner`: no owner holds the heads of more than 16 triples of one device's 512 slots; some owner holds exactly 16. `tail_owner`: no owner holds the tails of more than 16 triples of one device's 512 slots; some owner holds exactly 16. `neg_owner`: no owner holds more than 2 of one device's 16 negatives; some owner holds exactly 2. Each group's counts sum to 20480, and some device of each group is full.
All inputs are finite; a program needn't handle non-finite values.
Results may differ from the reference program's by a relative error of at most 0.0045.
Values may be sent and summed in bfloat16 or wider, within the bound.
No kernel may reach another device: no remote copies, remote signals or barrier semaphores. Data moves between devices by JAX's collectives and lax.ppermute only.
A program may use at most 64 MiB of HBM per device.

```python
import math
import jax
import jax.numpy as jnp
import numpy as np
from jax import lax

D = 512
REL = 4
TRI_DEV = 512
CLS_DEV = 2048
NEG = 1024
TRIPLES = 131072
NEG_DEV = 16
NEG_ALL = 4096
CLASSES = 131072
CAP = 16
CAP_N = 2
N_GRP = 4
N_SHARD = 64


def pattern_table(key):
    bits = jax.random.bernoulli(jax.random.fold_in(key, 7), 0.5, (NEG // 64, D))
    return jnp.where(bits, 1.0, -1.0).astype(jnp.float32)


def planted_triples(key):
    base = jax.random.fold_in(key, 11)
    flag = jax.random.randint(jax.random.fold_in(base, 1), (TRIPLES,), 0, 256) == 0
    which = jax.random.randint(jax.random.fold_in(base, 2), (TRIPLES,), 0, NEG // 64)
    amount = jax.random.uniform(jax.random.fold_in(base, 3), (TRIPLES,), jnp.float32, 0.45, 1.2)
    spacing = jax.random.uniform(jax.random.fold_in(base, 4), (TRIPLES,), jnp.float32, 1.6, 2.4)
    side = jnp.where(jax.random.bernoulli(jax.random.fold_in(base, 5), 0.5, (TRIPLES,)), 1.0, -1.0)
    return (flag, which, amount, spacing * side)


def normal_rows(key, count):
    return jnp.clip(0.3 * jax.random.normal(key, (count, D), jnp.float32), -2.0, 2.0)


def draw_head_vecs(key, part):
    noise_key = jax.random.fold_in(key, 21)
    values = normal_rows(noise_key, TRIPLES)
    flag, which, amount, spacing = planted_triples(key)
    table = pattern_table(key)
    planted = amount[:, None] * table[which]
    return jnp.where(flag[:, None], planted, values).astype(jnp.bfloat16)


def draw_tail_vecs(key, part):
    noise_key = jax.random.fold_in(key, 22)
    values = normal_rows(noise_key, TRIPLES)
    flag, which, amount, spacing = planted_triples(key)
    table = pattern_table(key)
    ripple = jax.random.uniform(jax.random.fold_in(key, 31), (TRIPLES, D), jnp.float32, -1.0, 1.0)
    level = 0.5 + spacing / (D * amount)
    planted = table[which] * (level[:, None] + 0.02 * ripple)
    return jnp.where(flag[:, None], planted, values).astype(jnp.bfloat16)


def draw_neg_vecs(key, part):
    noise_key = jax.random.fold_in(key, 23)
    values = normal_rows(noise_key, NEG_ALL)
    rows = jnp.arange(NEG_ALL, dtype=jnp.int32)
    group = rows // NEG
    within = rows % NEG
    offset = jax.random.randint(jax.random.fold_in(key, 41), (NEG_ALL // NEG,), 0, 64)
    flag = within % 64 == offset[group]
    table = pattern_table(key)
    planted = 0.5 * table[within // 64]
    return jnp.where(flag[:, None], planted, values).astype(jnp.bfloat16)


def draw_relations(key, part):
    noise_key = jax.random.fold_in(key, 24)
    noise = 0.5 * D ** (-0.5) * jax.random.normal(noise_key, (REL, D, D), jnp.float32)
    noise = jnp.clip(noise, -0.09, 0.09)
    eye = jnp.eye(D, dtype=jnp.float32)
    return (eye[None, :, :] + noise).astype(jnp.bfloat16)


def with_ends(drawn, key, low, largest):
    extent = drawn.shape
    spot = [jax.random.randint(jax.random.fold_in(key, axis), (), 0, extent[axis]) for axis in range(len(extent))]
    drawn = drawn.at[tuple(spot)].set(low)
    longest = extent.index(max(extent))
    spot[longest] = (spot[longest] + 1) % extent[longest]
    return drawn.at[tuple(spot)].set(largest)


def length_profile(count, total, reach, slope):
    weights = [(1 << 20) // math.isqrt(rank ** slope) + 1 for rank in range(2, count + 1)]
    surplus, holding = total - reach - (count - 1), [1] * (count - 1)
    while surplus > 0:
        candidates = [i for i in range(count - 1) if holding[i] < reach]
        whole, budget = sum([weights[i] for i in candidates]), surplus
        for i in candidates:
            addition = min(reach - holding[i], max(1, budget * weights[i] // whole), surplus)
            holding[i] = holding[i] + addition
            surplus = surplus - addition
    return np.array([reach] + holding)


def ragged(stream_key, number_of, total, limit, slope):
    if number_of == 2:
        one = jax.random.randint(stream_key, (), max(1, total - limit), min(limit, total - 1) + 1)
        return jnp.stack([one, total - one])
    lengths = jnp.asarray(length_profile(number_of, total, limit, slope), jnp.int32)
    pairs = (number_of - 1) // 2
    donor, taker = lengths[1:1 + 2 * pairs:2], lengths[2:2 + 2 * pairs:2]
    margin = jnp.minimum(donor - 1, limit - taker)
    moved = jax.random.randint(jax.random.fold_in(stream_key, 1), (pairs,), 0, 1 << 20) % (margin + 1)
    lengths = lengths.at[1:1 + 2 * pairs:2].set(donor - moved).at[2:2 + 2 * pairs:2].set(taker + moved)
    return lengths[jax.random.permutation(jax.random.fold_in(stream_key, 2), number_of)]


def assign_block(stream_key, own, number, rows, number_of, top, most, lean):
    order = jax.random.permutation(stream_key, number_of)
    heavy_load, ordinary = portions_of(number_of, rows * top, most, lean, True), portions_of(number_of, rows * top, most, lean, False)
    places = jnp.arange(number_of)

    def named(tallies, turn):
        used = int((tallies > 0).sum())
        fixed = max(1, used // 4)
        moved = fixed + (places - fixed + turn * (used - fixed)) % max(1, number_of - fixed)
        return jnp.zeros((number_of,), jnp.int32).at[order[jnp.where(places < fixed, places, moved)]].set(jnp.asarray(tallies, jnp.int32))

    tallies = jnp.where(number % 4 == 0, named(heavy_load, number // 4), named(ordinary, number - number // 4 - 1))
    mixed = jax.random.permutation(jax.random.fold_in(own, 3), number_of)
    donor, taker = mixed[0:number_of // 2 * 2:2], mixed[1:number_of // 2 * 2:2]
    margin = jnp.minimum(tallies[donor] - 1, most - tallies[taker]) // 2
    margin = jnp.where((donor == order[0]) | (taker == order[0]) | (tallies[taker] == 0), 0, jnp.maximum(margin, 0))
    moved = jax.random.randint(jax.random.fold_in(own, 4), (number_of // 2,), 0, 1 << 20) % (margin + 1)
    tallies = tallies.at[donor].add(-moved).at[taker].add(moved)
    items = jnp.searchsorted(jnp.cumsum(tallies), jnp.arange(rows * top), side="right").astype(jnp.int32)
    listing = items.reshape(top, rows).T
    listing = listing[jax.random.permutation(jax.random.fold_in(own, 1), rows)]
    turn = jax.random.randint(jax.random.fold_in(own, 2), (rows, 1), 0, top)
    return jnp.take_along_axis(listing, (jnp.arange(top)[None, :] + turn) % top, axis=1)


def portions_of(count, total, reach, slope, full):
    portions = [(1 << 20) // math.isqrt(grade ** slope) + 1 for grade in range(1, count + 1)]
    largest = reach if full else min(reach, max(-(-total // count), total * portions[0] // sum(portions)))
    least = 1 if total - largest >= count - 1 else 0
    holding, rest = [largest] + [least] * (count - 1), total - largest - least * (count - 1)
    while rest > 0:
        free = [i for i in range(1, count) if holding[i] < largest] or [i for i in range(1, count) if holding[i] < reach]
        mass, budget = sum([portions[i] for i in free]), rest
        for i in free:
            addition = min(reach - holding[i], max(1, budget * portions[i] // mass), rest)
            holding[i] = holding[i] + addition
            rest = rest - addition
    return np.array(holding)


def setup_inputs(seed: int = 0) -> dict:
    splits = jax.random.split(jax.random.key(seed), 13)
    head_vecs = draw_head_vecs(jax.random.fold_in(splits[12], 71), 0)
    tail_vecs = draw_tail_vecs(jax.random.fold_in(splits[12], 71), 0)
    rel_id = with_ends(jax.random.randint(splits[2], (TRIPLES,), 0, REL), jax.random.fold_in(splits[2], 1), 0, REL - 1).astype(jnp.int32)
    head_owner_keys = jax.random.split(jax.random.fold_in(splits[3], 1), TRIPLES // TRI_DEV)
    head_owner_turns = jax.random.permutation(jax.random.fold_in(splits[3], 3), TRIPLES // TRI_DEV)
    head_owner = jax.vmap(lambda own, number: assign_block(jax.random.fold_in(splits[3], 2), own, number, TRI_DEV, N_SHARD, 1, CAP, 2))(head_owner_keys, head_owner_turns).reshape((TRIPLES, 1))
    head_row = with_ends(jax.random.randint(splits[4], (TRIPLES,), 0, CLS_DEV), jax.random.fold_in(splits[4], 1), 0, CLS_DEV - 1).astype(jnp.int32)
    tail_owner_keys = jax.random.split(jax.random.fold_in(splits[5], 1), TRIPLES // TRI_DEV)
    tail_owner_turns = jax.random.permutation(jax.random.fold_in(splits[5], 3), TRIPLES // TRI_DEV)
    tail_owner = jax.vmap(lambda own, number: assign_block(jax.random.fold_in(splits[5], 2), own, number, TRI_DEV, N_SHARD, 1, CAP, 2))(tail_owner_keys, tail_owner_turns).reshape((TRIPLES, 1))
    tail_row = with_ends(jax.random.randint(splits[6], (TRIPLES,), 0, CLS_DEV), jax.random.fold_in(splits[6], 1), 0, CLS_DEV - 1).astype(jnp.int32)
    neg_vecs = draw_neg_vecs(jax.random.fold_in(splits[12], 71), 0)
    neg_owner_keys = jax.random.split(jax.random.fold_in(splits[8], 1), NEG_ALL // NEG_DEV)
    neg_owner_turns = jax.random.permutation(jax.random.fold_in(splits[8], 3), NEG_ALL // NEG_DEV)
    neg_owner = jax.vmap(lambda own, number: assign_block(jax.random.fold_in(splits[8], 2), own, number, NEG_DEV, N_SHARD, 1, CAP_N, 1))(neg_owner_keys, neg_owner_turns).reshape((NEG_ALL, 1))
    neg_row = with_ends(jax.random.randint(splits[9], (NEG_ALL,), 0, CLS_DEV), jax.random.fold_in(splits[9], 1), 0, CLS_DEV - 1).astype(jnp.int32)
    counts = jax.vmap(lambda own: ragged(own, N_SHARD, N_SHARD * TRI_DEV * 5 // 8, TRI_DEV, 2))(jax.random.split(splits[10], N_GRP)).reshape((N_GRP, N_SHARD)).astype(jnp.int32)
    relations = draw_relations(jax.random.fold_in(splits[12], 71), 0)
    return {"head_vecs": head_vecs, "tail_vecs": tail_vecs, "rel_id": rel_id, "head_owner": head_owner, "head_row": head_row, "tail_owner": tail_owner, "tail_row": tail_row, "neg_vecs": neg_vecs, "neg_owner": neg_owner, "neg_row": neg_row, "counts": counts, "relations": relations}


def relation_apply(vectors, relation_ids, relations, transpose):
    result = jnp.zeros((vectors.shape[0], relations.shape[2]), jnp.float32)
    contract = 2 if transpose else 1
    for index in range(relations.shape[0]):
        product = lax.dot_general(vectors, relations[index], (((1,), (contract - 1 if transpose else 0,)), ((), ())), preferred_element_type=jnp.float32)
        result = result + jnp.where((relation_ids == index)[:, None], product, 0.0)
    return result


def score_weights(query, tails, negatives, live):
    positive = jnp.sum(query.astype(jnp.float32) * tails.astype(jnp.float32), axis=1)
    scores = lax.dot_general(query, negatives, (((1,), (1,)), ((), ())), preferred_element_type=jnp.float32)
    top = jnp.maximum(positive, jnp.max(scores, axis=1))
    pos_exp = jnp.exp(positive - top)
    neg_exp = jnp.exp(scores - top[:, None])
    total = pos_exp + jnp.sum(neg_exp, axis=1)
    gpos = jnp.where(live, pos_exp / total - 1.0, 0.0)
    gneg = jnp.where(live[:, None], neg_exp / total[:, None], 0.0).astype(jnp.bfloat16)
    return gpos, gneg


def reference(head_vecs, tail_vecs, rel_id, head_owner, head_row, tail_owner, tail_row, neg_vecs, neg_owner, neg_row, counts, relations):
    query = relation_apply(head_vecs, rel_id, relations, False).astype(jnp.bfloat16)
    slots = jnp.arange(TRIPLES, dtype=jnp.int32)
    device = slots // TRI_DEV
    live = (slots % TRI_DEV) < counts.reshape(-1)[device]
    per_group = TRI_DEV * N_SHARD
    dquery_parts = []
    dtail_parts = []
    dneg_parts = []
    for group in range(N_GRP):
        lo = group * per_group
        hi = lo + per_group
        negatives = neg_vecs[group * NEG:(group + 1) * NEG]
        gpos, gneg = score_weights(query[lo:hi], tail_vecs[lo:hi], negatives, live[lo:hi])
        dquery = gpos[:, None] * tail_vecs[lo:hi].astype(jnp.float32) + jnp.dot(gneg, negatives, preferred_element_type=jnp.float32)
        dquery_parts.append(dquery.astype(jnp.bfloat16))
        dtail_parts.append(gpos[:, None] * query[lo:hi].astype(jnp.float32))
        dneg_parts.append(lax.dot_general(gneg, query[lo:hi], (((0,), (0,)), ((), ())), preferred_element_type=jnp.float32))
    dquery = jnp.concatenate(dquery_parts, axis=0)
    dtail = jnp.concatenate(dtail_parts, axis=0)
    dnegative = jnp.concatenate(dneg_parts, axis=0)
    dhead = relation_apply(dquery, rel_id, relations, True)
    triple_group = (slots // per_group).astype(jnp.int32)
    neg_group = (jnp.arange(NEG_ALL, dtype=jnp.int32) // NEG).astype(jnp.int32)
    head_ids = triple_group * CLASSES + head_owner[:, 0] * CLS_DEV + head_row
    tail_ids = triple_group * CLASSES + tail_owner[:, 0] * CLS_DEV + tail_row
    neg_ids = neg_group * CLASSES + neg_owner[:, 0] * CLS_DEV + neg_row
    rows = jnp.concatenate([dhead, dtail, dnegative], axis=0)
    ids = jnp.concatenate([head_ids, tail_ids, neg_ids], axis=0).astype(jnp.int32)
    entity_grad = jax.ops.segment_sum(rows, ids, num_segments=N_GRP * CLASSES).reshape(N_GRP, CLASSES, D)
    blocks = []
    for index in range(REL):
        masked = jnp.where((rel_id == index)[:, None], dquery, jnp.zeros_like(dquery))
        blocks.append(lax.dot_general(head_vecs, masked, (((0,), (0,)), ((), ())), preferred_element_type=jnp.float32))
    relation_grad = jnp.concatenate(blocks, axis=0)
    return entity_grad, relation_grad
```

```python
import jax
import jax.numpy as jnp
from jax import lax
from jax.experimental import pallas as pl
from jax.experimental.pallas import tpu as pltpu
from jax.sharding import Mesh, PartitionSpec as P

CLS_DEV = 2048
CAP = 16
CAP_N = 2
SIZES = {"y": 4, "z": 8, "x": 4, "c": 2}
SHARD = ("z", "x", "c")
ALL = ("y",) + SHARD
BF = jnp.bfloat16
F32 = jnp.float32


def swap(a, axis, flip):
    return lax.ppermute(a, axis, [(i, i ^ flip) for i in range(SIZES[axis])])


def ring_halves(blocks, axis, dtypes):
    me = lax.axis_index(axis)
    inner = (me == 1) | (me == 2)
    outer_set = jnp.stack([blocks[0], blocks[3]])
    inner_set = jnp.stack([blocks[1], blocks[2]])
    keep = jnp.where(inner, inner_set, outer_set)
    send = jnp.where(inner, outer_set, inner_set).astype(dtypes[0])
    keep = keep + swap(send, axis, 1).astype(F32)
    low = me < 2
    send = jnp.where(low, keep[1], keep[0]).astype(dtypes[1])
    return jnp.where(low, keep[0], keep[1]) + swap(send, axis, 3).astype(F32)


def cube_halves(blocks):
    me = lax.axis_index("z")
    for flip in (4, 2, 1):
        half = blocks.shape[0] // 2
        high = (me & flip) != 0
        send = jnp.where(high, blocks[:half], blocks[half:])
        keep = jnp.where(high, blocks[half:], blocks[:half])
        blocks = keep + swap(send, "z", flip)
    return blocks[0]


def slots_of(owners, cap):
    n = owners.shape[0]
    column = owners
    row = owners.reshape(1, n)
    before = lax.broadcasted_iota(jnp.int32, (n, n), 0) < lax.broadcasted_iota(jnp.int32, (n, n), 1)
    rank = jnp.sum(jnp.where((column == row) & before, 1, 0), axis=0, keepdims=True)
    return row * cap + rank


def onehot_of(slots, count):
    return lax.broadcasted_iota(jnp.int32, (count, slots.shape[1]), 0) == slots


def pick(hot, values):
    return jnp.sum(jnp.where(hot, values.reshape(1, -1), 0), axis=1)


def combine_kernel(tail_ref, head_ref, neg_ref, tl_ref, hl_ref, nl_ref, gp_ref, out_ref):
    rows = out_ref.shape[0]
    first = pl.program_id(0) * rows

    def hot(labels, weights):
        ids = lax.broadcasted_iota(jnp.int32, (rows, labels.shape[1]), 0) + first
        return jnp.where(ids == labels, weights, 0.0).astype(BF)

    total = jnp.dot(hot(tl_ref[...], gp_ref[...]), tail_ref[...], preferred_element_type=F32)
    total += jnp.dot(hot(hl_ref[...], 1.0), head_ref[...], preferred_element_type=F32)
    total += jnp.dot(hot(nl_ref[...], 1.0), neg_ref[...], preferred_element_type=F32)
    out_ref[...] = total


def combine(tails, heads, negs, tail_ids, head_ids, neg_ids, gpos):
    tile = 256
    args = (tails, heads, negs, tail_ids, head_ids, neg_ids, gpos)
    whole = lambda a: pl.BlockSpec(a.shape, lambda i: (0, 0))
    return pl.pallas_call(
        combine_kernel,
        grid=(CLS_DEV // tile,),
        in_specs=[whole(a) for a in args],
        out_specs=pl.BlockSpec((tile, tails.shape[1]), lambda i: (i, 0)),
        out_shape=jax.ShapeDtypeStruct((CLS_DEV, tails.shape[1]), F32),
        compiler_params=pltpu.CompilerParams(vmem_limit_bytes=40 * 2**20),
        name="combine",
    )(*args)


def on_device(
    head_vecs, tail_vecs, rel_id, head_owner, head_row, tail_owner, tail_row,
    neg_vecs, neg_owner, neg_row, counts, relations,
):
    n, width = head_vecs.shape
    rels = relations.shape[0]
    owners = SIZES["z"] * SIZES["x"] * SIZES["c"]
    core = lax.axis_index("c")

    with jax.named_scope("gather_negatives"):
        wide = jnp.broadcast_to(neg_vecs[None], (owners // 2,) + neg_vecs.shape)
        near = lax.all_to_all(wide, ("z", "x"), 0, 0, tiled=True).reshape(-1, width)
        negatives = jnp.concatenate([near, swap(near, "c", 1)], axis=0)

    with jax.named_scope("query"):
        of_rel = [(rel_id == r)[:, None] for r in range(rels)]
        spread = lambda v: jnp.concatenate([jnp.where(m, v, jnp.zeros_like(v)) for m in of_rel], axis=1)
        query = jnp.dot(spread(head_vecs), relations.reshape(rels * width, width), preferred_element_type=F32).astype(BF)
    with jax.named_scope("pack_tails"):
        tail_hot = onehot_of(slots_of(tail_owner, CAP), owners * CAP)
        tail_rows = jnp.dot(tail_hot.astype(BF), query, preferred_element_type=F32).astype(BF)
        got_tails = lax.all_to_all(tail_rows.reshape(owners, CAP, width), SHARD, 0, 0, tiled=True)

    with jax.named_scope("weights"):
        live = jnp.arange(n, dtype=jnp.int32) < counts[0, 0]
        positive = jnp.sum(query.astype(F32) * tail_vecs.astype(F32), axis=1)
        scores = lax.dot_general(query, negatives, (((1,), (1,)), ((), ())), preferred_element_type=F32)
        top = jnp.maximum(positive, jnp.max(scores, axis=1))
        pos_exp = jnp.exp(positive - top)
        neg_exp = jnp.exp(scores - top[:, None])
        total = pos_exp + jnp.sum(neg_exp, axis=1)
        gpos = jnp.where(live, pos_exp / total - 1.0, 0.0)
        gneg = jnp.where(live[:, None], neg_exp / total[:, None], 0.0).astype(BF)
    with jax.named_scope("dquery"):
        dquery = (
            gpos[:, None] * tail_vecs.astype(F32) + jnp.dot(gneg, negatives, preferred_element_type=F32)
        ).astype(BF)
        by_rel = spread(dquery)
    with jax.named_scope("pack_heads"):
        dhead = lax.dot_general(
            by_rel.reshape(n, rels, width), relations, (((1, 2), (0, 2)), ((), ())), preferred_element_type=F32
        ).astype(BF)
        head_hot = onehot_of(slots_of(head_owner, CAP), owners * CAP)
        head_rows = jnp.dot(head_hot.astype(BF), dhead, preferred_element_type=F32).astype(BF)
        got_heads = lax.all_to_all(head_rows.reshape(owners, CAP, width), SHARD, 0, 0, tiled=True)

    with jax.named_scope("neg_terms"):
        neg_terms = lax.dot_general(gneg, query, (((0,), (0,)), ((), ())), preferred_element_type=F32)
        half = neg_terms.shape[0] // 2
        own = neg_terms[:half] + swap(neg_terms[half:].astype(BF), "c", 1).astype(F32)
        own = own.reshape(8, 4, -1, width).transpose(1, 0, 2, 3)
        neg_grad = cube_halves(ring_halves(own, "x", (BF, F32)))
    with jax.named_scope("rel_terms"):
        rel_terms = lax.dot_general(head_vecs, by_rel, (((0,), (0,)), ((), ())), preferred_element_type=F32)
        cut = rel_terms.reshape(8, 4, 2, 8, rels * width)
        first, second = cut[:, :, 0], cut[:, :, 1]
        mine = jnp.where(core == 0, first, second)
        other = jnp.where(core == 0, second, first).astype(BF)
        mine = mine + swap(other, "c", 1).astype(F32)
        mine = jnp.stack([mine[..., r * width:(r + 1) * width] for r in range(rels)])
        mine = ring_halves(mine, "y", (BF, BF))
        relation_grad = cube_halves(ring_halves(mine.transpose(1, 0, 2, 3), "x", (F32, F32)))

    with jax.named_scope("small"):
        neg_hot = onehot_of(slots_of(neg_owner, CAP_N), owners * CAP_N)
        neg_rows = jnp.dot(neg_hot.astype(BF), neg_grad.astype(BF), preferred_element_type=F32).astype(BF)
        ids = [
            pick(hot, rows + 1).reshape(owners, -1)
            for hot, rows in ((tail_hot, tail_row), (head_hot, head_row), (neg_hot, neg_row))
        ]
        gp = pick(tail_hot, gpos).reshape(owners, CAP)
        gp_top = gp.astype(BF)
        extras = [(i >> 7).astype(BF) for i in ids] + [(i & 127).astype(BF) for i in ids]
        extras += [gp_top, (gp - gp_top.astype(F32)).astype(BF)]
        sizes = [e.shape[1] for e in extras]
        line = jnp.concatenate(extras, axis=1)
        line = jnp.pad(line, ((0, 0), (0, 1024 - line.shape[1])))
        packed = jnp.concatenate([neg_rows.reshape(owners, 8, 128), line.reshape(owners, 8, 128)], axis=1)
        got = lax.all_to_all(packed, SHARD, 0, 0, tiled=True)
        got_negs = got[:, :8].reshape(owners * CAP_N, width)
        line = got[:, 8:10].reshape(owners, 256).astype(F32)
        parts, at = [], 0
        for s in sizes:
            parts.append(line[:, at:at + s].reshape(1, -1))
            at += s
        got_ids = [(parts[i] * 128 + parts[i + 3]).astype(jnp.int32) - 1 for i in range(3)]
        got_gpos = parts[6] + parts[7]
    with jax.named_scope("combine"):
        owned = combine(
            got_tails.reshape(-1, width), got_heads.reshape(-1, width), got_negs,
            got_ids[0], got_ids[1], got_ids[2], got_gpos,
        )
    return owned[None], relation_grad


def solution(mesh):
    fine = Mesh(mesh.devices.reshape(*SIZES.values()), tuple(SIZES))
    whole = P(ALL)
    wide = P(ALL, None)
    return jax.shard_map(
        on_device,
        mesh=fine,
        in_specs=(
            wide, wide, whole, wide, whole, wide, whole, wide, wide, whole, P("y", SHARD), P(),
        ),
        out_specs=(P("y", SHARD, None), wide),
        check_vma=False,
    )
```

```python
import jax
import jax.numpy as jnp
from jax import lax
from jax.experimental import pallas as pl
from jax.experimental.pallas import tpu as pltpu
from jax.sharding import Mesh, PartitionSpec as P

CLS_DEV = 2048
CAP = 16
CAP_N = 2
SIZES = {"y": 4, "z": 8, "x": 4, "c": 2}
SHARD = ("z", "x", "c")
ALL = ("y",) + SHARD
BF = jnp.bfloat16
F32 = jnp.float32


def swap(a, axis, flip):
    return lax.ppermute(a, axis, [(i, i ^ flip) for i in range(SIZES[axis])])


def pair_send(blocks):
    me = lax.axis_index("y")
    inner = (me == 1) | (me == 2)
    outer_set = jnp.stack([blocks[0], blocks[3]])
    inner_set = jnp.stack([blocks[1], blocks[2]])
    return jnp.where(inner, outer_set, inner_set).astype(BF), jnp.where(inner, inner_set, outer_set)


def pair_keep(arrived, keep):
    keep = keep + arrived.astype(F32)
    low = lax.axis_index("y") < 2
    send = jnp.where(low, keep[1], keep[0]).astype(BF)
    return jnp.where(low, keep[0], keep[1]) + swap(send, "y", 3).astype(F32)


def column_sum(own, dtype):
    me = lax.axis_index("x")
    block = lambda flip: lax.dynamic_index_in_dim(own, me ^ flip, 1, keepdims=False)
    moved = [swap(block(flip).astype(dtype), "x", flip).astype(F32) for flip in (1, 3, 2)]
    return block(0) + moved[0] + moved[1] + moved[2]


def slots_of(owners, cap):
    n = owners.shape[0]
    column = owners
    row = owners.reshape(1, n)
    before = lax.broadcasted_iota(jnp.int32, (n, n), 0) < lax.broadcasted_iota(jnp.int32, (n, n), 1)
    rank = jnp.sum(jnp.where((column == row) & before, 1, 0), axis=0, keepdims=True)
    return row * cap + rank


def onehot_of(slots, count):
    return lax.broadcasted_iota(jnp.int32, (count, slots.shape[1]), 0) == slots


def pick(hot, values):
    return jnp.sum(jnp.where(hot, values.reshape(1, -1), 0), axis=1)


def heads_kernel(dquery_ref, rel_ref, relations_ref, slots_ref, out_ref):
    owners = out_ref.shape[0]
    dquery = dquery_ref[...]
    dhead = jnp.zeros(dquery.shape, F32)
    for r in range(relations_ref.shape[0]):
        masked = jnp.where(rel_ref[...] == r, dquery.astype(F32), 0.0).astype(BF)
        dhead += lax.dot_general(masked, relations_ref[r], (((1,), (1,)), ((), ())), preferred_element_type=F32)
    hot = onehot_of(slots_ref[...], owners * CAP)
    rows = jnp.dot(jnp.where(hot, 1.0, 0.0).astype(BF), dhead.astype(BF), preferred_element_type=F32).astype(BF)
    for block in range(4):
        out_ref[:, block * CAP:(block + 1) * CAP, :] = rows[:, block * 128:(block + 1) * 128].reshape(owners, CAP, 128)


def pack_heads(dquery, rel_id, relations, slots, owners):
    return pl.pallas_call(
        heads_kernel,
        out_shape=jax.ShapeDtypeStruct((owners, 4 * CAP, 128), BF),
        compiler_params=pltpu.CompilerParams(vmem_limit_bytes=32 * 2**20),
        name="pack_heads",
    )(dquery, rel_id, relations, slots)


def finish_kernel(terms_ref, slots_ref, heads_ref, line_ref, out_ref):
    owners = out_ref.shape[0]
    grad = jnp.sum(terms_ref[...].astype(F32), axis=0).astype(BF)
    count = grad.shape[0]
    entry = lax.broadcasted_iota(jnp.int32, (owners * 8, count), 0)
    filled = (entry // 8) * CAP_N + entry % CAP_N == slots_ref[...]
    column = (entry % 8) // CAP_N
    rows = jnp.zeros((owners * 8, 128), F32)
    for block in range(4):
        hot = jnp.where(filled & (column == block), 1.0, 0.0).astype(BF)
        rows += jnp.dot(hot, grad[:, block * 128:(block + 1) * 128], preferred_element_type=F32)
    out_ref[:, :64, :] = heads_ref[...]
    small = jnp.concatenate([rows.reshape(owners, 8, 128), line_ref[...].astype(F32)], axis=1)
    out_ref[:, 64:, :] = small.astype(BF)


def finish(terms, slots, heads, line):
    args = (terms, slots, heads, line)
    return pl.pallas_call(
        finish_kernel,
        out_shape=jax.ShapeDtypeStruct((heads.shape[0], 80, 128), BF),
        compiler_params=pltpu.CompilerParams(vmem_limit_bytes=32 * 2**20),
        name="finish",
    )(*args)


FIELDS = dict(tail_hi=0, head_hi=16, neg_hi=32, tail_lo=34, head_lo=50, neg_lo=66, gpos_hi=68, gpos_lo=84)


def combine_kernel(tail_ref, got_ref, out_ref, head_rows, tail_ids, head_ids, neg_ids, gpos):
    owners = got_ref.shape[0]
    rows = out_ref.shape[0]

    @pl.when(pl.program_id(0) == 0)
    def _():
        for block in range(4):
            head_rows[:, block * 128:(block + 1) * 128] = got_ref[:, block * CAP:(block + 1) * CAP, :].reshape(-1, 128)
        line = got_ref[:, 72:80, :].astype(F32)[:, 0, :].astype(BF)

        def spread(high, low, scale, per, cap):
            total = owners * per
            field = lax.broadcasted_iota(jnp.int32, (128, total), 0)
            place = lax.broadcasted_iota(jnp.int32, (128, total), 1) % cap
            take = jnp.where(field == FIELDS[high] + place, scale, 0.0) + jnp.where(field == FIELDS[low] + place, 1.0, 0.0)
            every = jnp.dot(line, take.astype(BF), preferred_element_type=F32)
            mine = lax.broadcasted_iota(jnp.int32, (owners, total), 1) // per
            mine = mine == lax.broadcasted_iota(jnp.int32, (owners, total), 0)
            return jnp.sum(jnp.where(mine, every, 0.0), axis=0, keepdims=True)

        tail_ids[...] = spread("tail_hi", "tail_lo", 128.0, CAP, CAP).astype(jnp.int32) - 1
        head_ids[...] = spread("head_hi", "head_lo", 128.0, CAP, CAP).astype(jnp.int32) - 1
        gpos[...] = spread("gpos_hi", "gpos_lo", 1.0, CAP, CAP)
        ids = spread("neg_hi", "neg_lo", 128.0, 8, CAP_N).astype(jnp.int32) - 1
        column = (lax.broadcasted_iota(jnp.int32, (4, owners * 8), 1) % 8) // CAP_N
        neg_ids[...] = jnp.where(column == lax.broadcasted_iota(jnp.int32, (4, owners * 8), 0), ids, -1)

    first = pl.program_id(0) * rows

    def hot(labels, weights):
        ids = lax.broadcasted_iota(jnp.int32, (rows, labels.shape[1]), 0) + first
        return jnp.where(ids == labels, weights, 0.0).astype(BF)

    negs = got_ref[:, 64:72, :].reshape(owners * 8, 128)
    total = jnp.dot(hot(tail_ids[...], gpos[...]), tail_ref[...], preferred_element_type=F32)
    total += jnp.dot(hot(head_ids[...], 1.0), head_rows[...], preferred_element_type=F32)
    parts = [jnp.dot(hot(neg_ids[block:block + 1, :], 1.0), negs, preferred_element_type=F32) for block in range(4)]
    out_ref[...] = total + jnp.concatenate(parts, axis=1)


def combine(tails, got):
    tile = 256
    width = tails.shape[1]
    return pl.pallas_call(
        combine_kernel,
        grid=(CLS_DEV // tile,),
        in_specs=[pl.BlockSpec(tails.shape, lambda i: (0, 0)), pl.BlockSpec(got.shape, lambda i: (0, 0, 0))],
        out_specs=pl.BlockSpec((tile, width), lambda i: (i, 0)),
        out_shape=jax.ShapeDtypeStruct((CLS_DEV, width), F32),
        scratch_shapes=[
            pltpu.VMEM(tails.shape, BF),
            pltpu.VMEM((1, tails.shape[0]), jnp.int32),
            pltpu.VMEM((1, tails.shape[0]), jnp.int32),
            pltpu.VMEM((4, got.shape[0] * 8), jnp.int32),
            pltpu.VMEM((1, tails.shape[0]), F32),
        ],
        compiler_params=pltpu.CompilerParams(vmem_limit_bytes=40 * 2**20),
        name="combine",
    )(tails, got)


def on_device(
    head_vecs, tail_vecs, rel_id, head_owner, head_row, tail_owner, tail_row,
    neg_vecs, neg_owner, neg_row, counts, relations,
):
    n, width = head_vecs.shape
    rels = relations.shape[0]
    owners = SIZES["z"] * SIZES["x"] * SIZES["c"]
    core = lax.axis_index("c")

    with jax.named_scope("gather_negatives"):
        wide = jnp.broadcast_to(neg_vecs[None], (SIZES["z"],) + neg_vecs.shape)
        column = lax.all_to_all(wide, "z", 0, 0, tiled=True).reshape(-1, width)
        near = jnp.concatenate([column] + [swap(column, "x", flip) for flip in (1, 3, 2)], axis=0)

    with jax.named_scope("query"):
        of_rel = [(rel_id == r)[:, None] for r in range(rels)]
        spread = lambda v: jnp.concatenate([jnp.where(m, v, jnp.zeros_like(v)) for m in of_rel], axis=1)
        query = jnp.dot(spread(head_vecs), relations.reshape(rels * width, width), preferred_element_type=F32).astype(BF)
    with jax.named_scope("pack_tails"):
        tail_hot = onehot_of(slots_of(tail_owner, CAP), owners * CAP)
        tail_rows = jnp.dot(tail_hot.astype(BF), query, preferred_element_type=F32).astype(BF)
        near, tail_rows = lax.optimization_barrier((near, tail_rows))
        got_tails = lax.all_to_all(tail_rows.reshape(owners, CAP, width), SHARD, 0, 0, tiled=True)
        negatives = jnp.concatenate([near, swap(near, "c", 1)], axis=0)
    with jax.named_scope("rel_heads"):
        feature = lax.broadcasted_iota(jnp.int32, (width, width // 2), 0)
        place = lax.broadcasted_iota(jnp.int32, (width, width // 2), 1)
        wanted = (feature == place // 8 * 16 + core * 8 + place % 8).astype(BF)
        both = jnp.concatenate([head_vecs, swap(head_vecs, "c", 1)], axis=0)
        both = jnp.dot(both, wanted, preferred_element_type=F32).astype(BF)
        both_rel = jnp.concatenate([rel_id, swap(rel_id, "c", 1)])
        both = jnp.concatenate(
            [jnp.where((both_rel == r)[:, None], both, jnp.zeros_like(both)) for r in range(rels)], axis=1
        )

    with jax.named_scope("weights"):
        live = jnp.arange(n, dtype=jnp.int32) < counts[0, 0]
        positive = jnp.sum(query.astype(F32) * tail_vecs.astype(F32), axis=1)
        scores = lax.dot_general(query, negatives, (((1,), (1,)), ((), ())), preferred_element_type=F32)
        top = jnp.maximum(positive, jnp.max(scores, axis=1))
        pos_exp = jnp.exp(positive - top)
        neg_exp = jnp.exp(scores - top[:, None])
        total = pos_exp + jnp.sum(neg_exp, axis=1)
        gpos = jnp.where(live, pos_exp / total - 1.0, 0.0)
        gneg = jnp.where(live[:, None], neg_exp / total[:, None], 0.0).astype(BF)
    with jax.named_scope("dquery"):
        dquery = (
            gpos[:, None] * tail_vecs.astype(F32) + jnp.dot(gneg, negatives, preferred_element_type=F32)
        ).astype(BF)
    with jax.named_scope("neg_terms"):
        neg_terms = lax.dot_general(gneg, query, (((0,), (0,)), ((), ())), preferred_element_type=F32)
        half = neg_terms.shape[0] // 2
        own = neg_terms[:half] + swap(neg_terms[half:].astype(BF), "c", 1).astype(F32)
        dquery, own = lax.optimization_barrier((dquery, own))
        own = own.reshape(4, 8, -1, width)
        moved = [swap(own[at].astype(BF), "x", flip).astype(F32) for at, flip in ((1, 1), (2, 3), (3, 2))]
        own = (own[0] + moved[0] + moved[1] + moved[2]).astype(BF)
    with jax.named_scope("pack_heads"):
        head_slots = slots_of(head_owner, CAP)
        head_hot = onehot_of(head_slots, owners * CAP)
        head_rows = pack_heads(dquery, rel_id.reshape(n, 1), relations, head_slots, owners)
    with jax.named_scope("rel_terms"):
        both_dquery = jnp.concatenate([dquery, swap(dquery, "c", 1)], axis=0)
        mine = lax.dot_general(both, both_dquery, (((0,), (0,)), ((), ())), preferred_element_type=F32)
        mine, keep = pair_send(mine.reshape(rels, -1, width))
        mine = swap(mine, "y", 1)
    with jax.named_scope("line"):
        neg_slots = slots_of(neg_owner, CAP_N)
        neg_hot = onehot_of(neg_slots, owners * CAP_N)
        ids = [
            pick(hot, rows + 1).reshape(owners, -1)
            for hot, rows in ((tail_hot, tail_row), (head_hot, head_row), (neg_hot, neg_row))
        ]
        gp = pick(tail_hot, gpos).reshape(owners, CAP)
        gp_top = gp.astype(BF)
        fields = [(i >> 7).astype(BF) for i in ids] + [(i & 127).astype(BF) for i in ids]
        fields += [gp_top, (gp - gp_top.astype(F32)).astype(BF)]
        line = jnp.concatenate(fields, axis=1)
        line = jnp.pad(line, ((0, 0), (0, 1024 - line.shape[1]))).reshape(owners, 8, 128)
    own, got_tails, mine = lax.optimization_barrier((own, got_tails, mine))
    with jax.named_scope("neg_exchange"):
        got_negs = lax.all_to_all(own, "z", 0, 0, tiled=True)
    with jax.named_scope("send_heads"):
        got = lax.all_to_all(finish(got_negs, neg_slots, head_rows, line), SHARD, 0, 0, tiled=True)
    with jax.named_scope("rel_sum"):
        mine = pair_keep(mine, keep)
        mine = column_sum(mine.reshape(8, 4, 8, width), F32)
        mine, got = lax.optimization_barrier((mine, got))
        relation_grad = jnp.sum(lax.all_to_all(mine, "z", 0, 0, tiled=True), axis=0)
    with jax.named_scope("combine"):
        owned = combine(got_tails.reshape(-1, width), got)
    return owned[None], relation_grad


def solution(mesh):
    fine = Mesh(mesh.devices.reshape(*SIZES.values()), tuple(SIZES))
    whole = P(ALL)
    wide = P(ALL, None)
    return jax.shard_map(
        on_device,
        mesh=fine,
        in_specs=(
            wide, wide, whole, wide, whole, wide, whole, wide, wide, whole, P("y", SHARD), P(),
        ),
        out_specs=(P("y", SHARD, None), wide),
        check_vma=False,
    )
```

```python
import jax
import jax.numpy as jnp
from jax import lax
from jax.experimental import pallas as pl
from jax.experimental.pallas import tpu as pltpu
from jax.sharding import Mesh, PartitionSpec as P

CLS_DEV = 2048
CAP = 16
CAP_N = 2
SIZES = {"y": 4, "z": 8, "x": 4, "c": 2}
SHARD = ("z", "x", "c")
ALL = ("y",) + SHARD
BF = jnp.bfloat16
F32 = jnp.float32


def swap(a, axis, flip):
    return lax.ppermute(a, axis, [(i, i ^ flip) for i in range(SIZES[axis])])


def pair_keep(arrived, keep):
    keep = keep + arrived.astype(F32)
    low = lax.axis_index("y") < 2
    send = jnp.where(low, keep[1], keep[0]).astype(BF)
    return jnp.where(low, keep[0], keep[1]) + swap(send, "y", 3).astype(F32)


def column_sum(own, dtype):
    me = lax.axis_index("x")
    block = lambda flip: lax.dynamic_index_in_dim(own, me ^ flip, 1, keepdims=False)
    moved = [swap(block(flip).astype(dtype), "x", flip).astype(F32) for flip in (1, 3, 2)]
    return block(0) + moved[0] + moved[1] + moved[2]


def onehot_of(slots, count):
    return lax.broadcasted_iota(jnp.int32, (count, slots.shape[1]), 0) == slots


def eye(n):
    return lax.broadcasted_iota(jnp.int32, (n, n), 0) == lax.broadcasted_iota(jnp.int32, (n, n), 1)


def to_column(row):
    return jnp.sum(jnp.where(eye(row.shape[1]), row.astype(F32), 0.0), axis=1, keepdims=True)


def query_kernel(heads_ref, rel_ref, relations_ref, query_ref, column_ref):
    heads = heads_ref[...].astype(F32)
    rel = to_column(rel_ref[...])
    column_ref[...] = rel.astype(jnp.int32)
    total = jnp.zeros(heads.shape, F32)
    for r in range(relations_ref.shape[0]):
        masked = jnp.where(rel == r, heads, 0.0).astype(BF)
        total += jnp.dot(masked, relations_ref[r], preferred_element_type=F32)
    query_ref[...] = total.astype(BF)


def make_query(heads, rel_id, relations):
    n = heads.shape[0]
    return pl.pallas_call(
        query_kernel,
        out_shape=(jax.ShapeDtypeStruct(heads.shape, BF), jax.ShapeDtypeStruct((n, 1), jnp.int32)),
        compiler_params=pltpu.CompilerParams(vmem_limit_bytes=32 * 2**20),
        cost_estimate=pl.CostEstimate(flops=4 * 10**9, bytes_accessed=4 * 2**20, transcendentals=0),
        name="query",
    )(heads, rel_id.reshape(1, n), relations)


FIELDS = dict(head_hi=0, tail_hi=16, neg_hi=32, head_lo=34, tail_lo=50, neg_lo=66, gpos_hi=68, gpos_lo=84)


def slots_kernel(ho_ref, to_ref, no_ref, hr_ref, tr_ref, nr_ref, hs_ref, ts_ref, ns_ref, line_ref, rank_ref):
    owners = line_ref.shape[0]
    line = jnp.zeros((owners, 128), F32)
    kinds = (("head", CAP, ho_ref, hr_ref, hs_ref), ("tail", CAP, to_ref, tr_ref, ts_ref), ("neg", CAP_N, no_ref, nr_ref, ns_ref))
    for kind, cap, owner_ref, row_ref, slots_ref in kinds:
        column = owner_ref[...].astype(F32)
        n = column.shape[0]
        row = jnp.sum(jnp.where(eye(n), column, 0.0), axis=0, keepdims=True)
        down = lax.broadcasted_iota(jnp.int32, (n, n), 0)
        across = lax.broadcasted_iota(jnp.int32, (n, n), 1)
        same = column == row
        rank_row = jnp.sum(jnp.where(same & (down < across), 1.0, 0.0), axis=0, keepdims=True)
        rank = jnp.sum(jnp.where(same & (across < down), 1.0, 0.0), axis=1, keepdims=True).astype(jnp.int32)
        slots_ref[...] = (row * cap + rank_row).astype(jnp.int32)
        if kind == "tail":
            rank_ref[...] = rank
        value = to_column(row_ref[...]).astype(jnp.int32) + 1
        field = lax.broadcasted_iota(jnp.int32, (n, 128), 1)
        put = jnp.where(field == FIELDS[kind + "_hi"] + rank, (value >> 7).astype(F32), 0.0)
        put += jnp.where(field == FIELDS[kind + "_lo"] + rank, (value & 127).astype(F32), 0.0)
        hot = lax.broadcasted_iota(jnp.int32, (owners, n), 0) == row.astype(jnp.int32)
        line += jnp.dot(jnp.where(hot, 1.0, 0.0).astype(BF), put.astype(BF), preferred_element_type=F32)
    wide = jnp.broadcast_to(line[:, None, :], (owners, 8, 128))
    line_ref[...] = jnp.where(lax.broadcasted_iota(jnp.int32, wide.shape, 1) == 0, wide, 0.0).astype(BF)


def make_slots(columns, rows, owners):
    return pl.pallas_call(
        slots_kernel,
        out_shape=tuple(jax.ShapeDtypeStruct((1, c.shape[0]), jnp.int32) for c in columns)
        + (jax.ShapeDtypeStruct((owners, 8, 128), BF), jax.ShapeDtypeStruct(columns[1].shape, jnp.int32)),
        compiler_params=pltpu.CompilerParams(vmem_limit_bytes=32 * 2**20),
        cost_estimate=pl.CostEstimate(flops=4 * 10**9, bytes_accessed=2**20, transcendentals=0),
        name="slots",
    )(*columns, *[r.reshape(1, -1) for r in rows])


def weights_kernel(count_ref, query_ref, tail_ref, near_ref, far_ref, dquery_ref, gpos_ref, own_ref, other_ref):
    query, near, far = query_ref[...], near_ref[...], far_ref[...]
    tails = tail_ref[...].astype(F32)
    n = query.shape[0]
    scores = lambda negatives: lax.dot_general(query, negatives, (((1,), (1,)), ((), ())), preferred_element_type=F32)
    near_scores, far_scores = scores(near), scores(far)
    positive = jnp.sum(query.astype(F32) * tails, axis=1, keepdims=True)
    top = jnp.maximum(jnp.max(near_scores, axis=1, keepdims=True), jnp.max(far_scores, axis=1, keepdims=True))
    top = jnp.maximum(positive, top)
    pos_exp = jnp.exp(positive - top)
    near_exp, far_exp = jnp.exp(near_scores - top), jnp.exp(far_scores - top)
    total = pos_exp + jnp.sum(near_exp, axis=1, keepdims=True) + jnp.sum(far_exp, axis=1, keepdims=True)
    live = lax.broadcasted_iota(jnp.int32, (n, 1), 0) < count_ref[0, 0]
    gpos = jnp.where(live, pos_exp / total - 1.0, 0.0)
    share = jnp.where(live, 1.0 / total, 0.0)
    near_w, far_w = (near_exp * share).astype(BF), (far_exp * share).astype(BF)
    terms = lambda w: lax.dot_general(w, query, (((0,), (0,)), ((), ())), preferred_element_type=F32)
    other_ref[...] = terms(far_w).astype(BF)
    own_ref[...] = terms(near_w)
    dquery = gpos * tails + jnp.dot(near_w, near, preferred_element_type=F32)
    dquery_ref[...] = (dquery + jnp.dot(far_w, far, preferred_element_type=F32)).astype(BF)
    gpos_ref[...] = gpos


def weights(counts, query, tails, near, far):
    n, width = query.shape
    shape = lambda rows, dtype: jax.ShapeDtypeStruct((rows, width), dtype)
    m = near.shape[0]
    return pl.pallas_call(
        weights_kernel,
        in_specs=[pl.BlockSpec(memory_space=pltpu.SMEM)] + [pl.BlockSpec(memory_space=pltpu.VMEM)] * 4,
        out_shape=(shape(n, BF), jax.ShapeDtypeStruct((n, 1), F32), shape(m, F32), shape(m, BF)),
        compiler_params=pltpu.CompilerParams(vmem_limit_bytes=40 * 2**20),
        name="weights",
    )(counts, query, tails, near, far)


NEGS, LINE, SUB = 4 * CAP, 4 * CAP + 8, 4 * CAP + 16


def tails_kernel(query_ref, slots_ref, out_ref):
    hot = jnp.where(onehot_of(slots_ref[...], out_ref.shape[0]), 1.0, 0.0).astype(BF)
    out_ref[...] = jnp.dot(hot, query_ref[...], preferred_element_type=F32).astype(BF)


def pack_tails(query, slots, owners):
    return pl.pallas_call(
        tails_kernel,
        out_shape=jax.ShapeDtypeStruct((owners * CAP, query.shape[1]), BF),
        compiler_params=pltpu.CompilerParams(vmem_limit_bytes=32 * 2**20),
        cost_estimate=pl.CostEstimate(flops=10**9, bytes_accessed=2**20, transcendentals=0),
        name="pack_tails",
    )(query, slots)


def heads_kernel(dquery_ref, rel_ref, relations_ref, slots_ref, line_ref, gpos_ref, rank_ref, tail_slots_ref, out_ref):
    owners = out_ref.shape[0]
    dquery = dquery_ref[...].astype(F32)
    n = dquery.shape[0]
    dhead = jnp.zeros(dquery.shape, F32)
    for r in range(relations_ref.shape[0]):
        masked = jnp.where(rel_ref[...] == r, dquery, 0.0).astype(BF)
        dhead += lax.dot_general(masked, relations_ref[r], (((1,), (1,)), ((), ())), preferred_element_type=F32)
    hot = jnp.where(onehot_of(slots_ref[...], owners * CAP), 1.0, 0.0).astype(BF)
    rows = jnp.dot(hot, dhead.astype(BF), preferred_element_type=F32).astype(BF)
    for block in range(4):
        at = block * CAP
        out_ref[:, at:at + CAP, :] = rows[:, block * 128:(block + 1) * 128].reshape(owners, CAP, 128)
    gpos = gpos_ref[...]
    high = gpos.astype(BF).astype(F32)
    field = lax.broadcasted_iota(jnp.int32, (n, 128), 1)
    put = jnp.where(field == FIELDS["gpos_hi"] + rank_ref[...], high, 0.0)
    put += jnp.where(field == FIELDS["gpos_lo"] + rank_ref[...], gpos - high, 0.0)
    of_owner = lax.broadcasted_iota(jnp.int32, (owners, n), 0) == tail_slots_ref[...] // CAP
    extra = jnp.dot(jnp.where(of_owner, 1.0, 0.0).astype(BF), put.astype(BF), preferred_element_type=F32)
    wide = jnp.broadcast_to(extra[:, None, :], (owners, 8, 128))
    wide = jnp.where(lax.broadcasted_iota(jnp.int32, wide.shape, 1) == 0, wide, 0.0)
    line = (line_ref[...].astype(F32) + wide).astype(BF)
    out_ref[:, NEGS:, :] = jnp.concatenate([jnp.zeros((owners, 8, 128), F32), line.astype(F32)], axis=1).astype(BF)


def pack_heads(dquery, rel_id, relations, slots, line, gpos, rank, tail_slots):
    return pl.pallas_call(
        heads_kernel,
        out_shape=jax.ShapeDtypeStruct((line.shape[0], SUB, 128), BF),
        compiler_params=pltpu.CompilerParams(vmem_limit_bytes=40 * 2**20),
        name="pack_heads",
    )(dquery, rel_id, relations, slots, line, gpos, rank, tail_slots)


def negs_kernel(terms_ref, slots_ref, have_ref, out_ref):
    owners = out_ref.shape[0]
    grad = jnp.sum(terms_ref[...].astype(F32), axis=0).astype(BF)
    entry = lax.broadcasted_iota(jnp.int32, (owners * 8, grad.shape[0]), 0)
    filled = (entry // 8) * CAP_N + entry % CAP_N == slots_ref[...]
    column = (entry % 8) // CAP_N
    rows = jnp.zeros((owners * 8, 128), F32)
    for block in range(4):
        hot = jnp.where(filled & (column == block), 1.0, 0.0).astype(BF)
        rows += jnp.dot(hot, grad[:, block * 128:(block + 1) * 128], preferred_element_type=F32)
    out_ref[...] = rows.reshape(owners, 8, 128).astype(BF)


def pack_negs(terms, slots, have):
    return pl.pallas_call(
        negs_kernel,
        grid=(1,),
        in_specs=[
            pl.BlockSpec(terms.shape, lambda i: (0, 0, 0)),
            pl.BlockSpec(slots.shape, lambda i: (0, 0)),
            pl.BlockSpec(memory_space=pl.ANY),
        ],
        out_specs=pl.BlockSpec((have.shape[0], 8, 128), lambda i: (0, NEGS // 8, 0)),
        out_shape=jax.ShapeDtypeStruct(have.shape, BF),
        input_output_aliases={2: 0},
        name="pack_negs",
    )(terms, slots, have)


def relation_kernel(inner_ref, both_ref, rel_ref, far_rel_ref, dquery_ref, far_ref, send_ref, keep_ref):
    n = dquery_ref.shape[0]
    near_rel, far_rel = rel_ref[...], to_column(far_rel_ref[...]).astype(jnp.int32)
    near_dquery, far_dquery = dquery_ref[...], far_ref[...]
    inner = inner_ref[0, 0] == 1

    def terms(relation):
        def part(rel, heads, dquery):
            masked = jnp.where(rel == relation, heads.astype(F32), 0.0).astype(BF)
            return lax.dot_general(masked, dquery, (((0,), (0,)), ((), ())), preferred_element_type=F32)

        return part(near_rel, both_ref[:n, :], near_dquery) + part(far_rel, both_ref[n:, :], far_dquery)

    for at, (outer_one, inner_one) in enumerate(((0, 1), (3, 2))):
        outer_terms, inner_terms = terms(outer_one), terms(inner_one)
        send_ref[at] = jnp.where(inner, outer_terms, inner_terms).astype(BF)
        keep_ref[at] = jnp.where(inner, inner_terms, outer_terms)


def relation_terms(inner, both, rel, far_rel, dquery, far_dquery):
    shape = (2, both.shape[1], dquery.shape[1])
    return pl.pallas_call(
        relation_kernel,
        in_specs=[pl.BlockSpec(memory_space=pltpu.SMEM)] + [pl.BlockSpec(memory_space=pltpu.VMEM)] * 5,
        out_shape=(jax.ShapeDtypeStruct(shape, BF), jax.ShapeDtypeStruct(shape, F32)),
        compiler_params=pltpu.CompilerParams(vmem_limit_bytes=40 * 2**20),
        name="relation_terms",
    )(inner, both, rel, far_rel, dquery, far_dquery)


def spread_line(block, high, low, scale, cap):
    owners = block.shape[0]
    line = block.astype(F32)[:, 0, :].astype(BF)
    total = owners * cap
    field = lax.broadcasted_iota(jnp.int32, (128, total), 0)
    place = lax.broadcasted_iota(jnp.int32, (128, total), 1) % cap
    take = jnp.where(field == FIELDS[high] + place, scale, 0.0)
    take += jnp.where(field == FIELDS[low] + place, 1.0, 0.0)
    every = jnp.dot(line, take.astype(BF), preferred_element_type=F32)
    mine = lax.broadcasted_iota(jnp.int32, (owners, total), 1) // cap
    mine = mine == lax.broadcasted_iota(jnp.int32, (owners, total), 0)
    return jnp.sum(jnp.where(mine, every, 0.0), axis=0, keepdims=True)


def combine_kernel(tails_ref, got_ref, out_ref, rows_of, ids, weights_of):
    owners = got_ref.shape[0]
    slots, negs = owners * CAP, owners * CAP_N
    rows = out_ref.shape[0]

    @pl.when(pl.program_id(0) == 0)
    def _():
        for block in range(4):
            at = block * CAP
            rows_of[:slots, block * 128:(block + 1) * 128] = got_ref[:, at:at + CAP, :].reshape(slots, 128)
        packed = got_ref[:, NEGS:LINE, :].reshape(owners * 8, 128)
        entry = lax.broadcasted_iota(jnp.int32, (negs, owners * 8), 0)
        source = lax.broadcasted_iota(jnp.int32, (negs, owners * 8), 1)
        for block in range(4):
            take = jnp.where(source == entry // CAP_N * 8 + block * CAP_N + entry % CAP_N, 1.0, 0.0).astype(BF)
            rows_of[slots:, block * 128:(block + 1) * 128] = jnp.dot(take, packed, preferred_element_type=F32).astype(BF)
        line = got_ref[:, LINE:, :]
        for first, kind, cap in ((0, "head", CAP), (slots, "neg", CAP_N), (slots + negs, "tail", CAP)):
            row = spread_line(line, kind + "_hi", kind + "_lo", 128.0, cap)
            ids[:, first:first + owners * cap] = row.astype(jnp.int32) - 1
        weights_of[...] = spread_line(line, "gpos_hi", "gpos_lo", 1.0, CAP)

    first = pl.program_id(0) * rows
    labels = ids[...]
    here = (labels >= first) & (labels < first + rows)
    here = jnp.where(here, labels - first, -1).astype(F32).astype(BF)
    cut = slots + negs

    def hot(labels, weights):
        place = lax.broadcasted_iota(jnp.int32, (rows, labels.shape[1]), 0).astype(F32).astype(BF)
        return jnp.where(place == labels, weights, jnp.zeros((1, 1), BF))

    total = jnp.dot(hot(here[:, :cut], jnp.ones((1, 1), BF)), rows_of[...], preferred_element_type=F32)
    total += jnp.dot(hot(here[:, cut:], weights_of[...].astype(BF)), tails_ref[...], preferred_element_type=F32)
    out_ref[...] = total


def combine(tails, got):
    tile, width = 256, tails.shape[1]
    slots, negs = got.shape[0] * CAP, got.shape[0] * CAP_N
    return pl.pallas_call(
        combine_kernel,
        grid=(CLS_DEV // tile,),
        in_specs=[pl.BlockSpec(tails.shape, lambda i: (0, 0)), pl.BlockSpec(got.shape, lambda i: (0, 0, 0))],
        out_specs=pl.BlockSpec((tile, width), lambda i: (i, 0)),
        out_shape=jax.ShapeDtypeStruct((CLS_DEV, width), F32),
        scratch_shapes=[
            pltpu.VMEM((slots + negs, width), BF),
            pltpu.VMEM((1, 2 * slots + negs), jnp.int32),
            pltpu.VMEM((1, slots), F32),
        ],
        compiler_params=pltpu.CompilerParams(vmem_limit_bytes=40 * 2**20),
        cost_estimate=pl.CostEstimate(flops=8 * 10**9, bytes_accessed=8 * 2**20, transcendentals=0),
        name="combine",
    )(tails, got)


def on_device(
    head_vecs, tail_vecs, rel_id, head_owner, head_row, tail_owner, tail_row,
    neg_vecs, neg_owner, neg_row, counts, relations,
):
    n, width = head_vecs.shape
    rels = relations.shape[0]
    owners = SIZES["z"] * SIZES["x"] * SIZES["c"]
    core = lax.axis_index("c")

    with jax.named_scope("query"):
        query, rel_column = make_query(head_vecs, rel_id, relations)
    with jax.named_scope("slots"):
        *slots, line, tail_rank = make_slots(
            (head_owner, tail_owner, neg_owner), (head_row, tail_row, neg_row), owners
        )
    with jax.named_scope("gather_negatives"):
        wide = jnp.broadcast_to(neg_vecs[None], (SIZES["z"],) + neg_vecs.shape)
        column = lax.all_to_all(wide, "z", 0, 0, tiled=True).reshape(-1, width)
        tail_rows = pack_tails(query, slots[1], owners)
        column, tail_rows = lax.optimization_barrier((column, tail_rows))
        near = jnp.concatenate([column] + [swap(column, "x", flip) for flip in (1, 3, 2)], axis=0)
        near, tail_rows = lax.optimization_barrier((near, tail_rows))
        far = swap(near, "c", 1)
    with jax.named_scope("send_tails"):
        got_tails = lax.all_to_all(tail_rows.reshape(owners, CAP, width), SHARD, 0, 0, tiled=True)
    with jax.named_scope("rel_heads"):
        feature = lax.broadcasted_iota(jnp.int32, (width, width // 2), 0)
        place = lax.broadcasted_iota(jnp.int32, (width, width // 2), 1)
        wanted = (feature == place // 8 * 16 + core * 8 + place % 8).astype(BF)
        both = jnp.concatenate([head_vecs, swap(head_vecs, "c", 1)], axis=0)
        both = jnp.dot(both, wanted, preferred_element_type=F32).astype(BF)
        far_rel = swap(rel_id, "c", 1).reshape(1, n)
        row = lax.axis_index("y")
        inner = ((row == 1) | (row == 2)).astype(jnp.int32).reshape(1, 1)

    with jax.named_scope("weights"):
        dquery, gpos, own, other = weights(counts, query, tail_vecs, near, far)
    with jax.named_scope("neg_sum"):
        own = own + swap(other, "c", 1).astype(F32)
        own = own.reshape(4, 8, -1, width)
        moved = [swap(own[at].astype(BF), "x", flip).astype(F32) for at, flip in ((1, 1), (2, 3), (3, 2))]
        own = (own[0] + moved[0] + moved[1] + moved[2]).astype(BF)
    with jax.named_scope("pack_heads"):
        heads = pack_heads(dquery, rel_column, relations, slots[0], line, gpos, tail_rank, slots[1])
    with jax.named_scope("rel_sum"):
        mine, keep = relation_terms(inner, both, rel_column, far_rel, dquery, swap(dquery, "c", 1))
    own, got_tails, heads, mine, keep = lax.optimization_barrier((own, got_tails, heads, mine, keep))
    with jax.named_scope("neg_exchange"):
        terms = lax.all_to_all(own, "z", 0, 0, tiled=True)
    with jax.named_scope("rel_halves"):
        mine = swap(mine, "y", 1)
        terms, mine = lax.optimization_barrier((terms, mine))
    with jax.named_scope("send_heads"):
        got = lax.all_to_all(pack_negs(terms, slots[2], heads), SHARD, 0, 0, tiled=True)
    with jax.named_scope("rel_column"):
        mine = column_sum(pair_keep(mine, keep).reshape(8, 4, 8, width), F32)
        mine, got = lax.optimization_barrier((mine, got))
    with jax.named_scope("rel_end"):
        relation_grad = jnp.sum(lax.all_to_all(mine, "z", 0, 0, tiled=True), axis=0)
    with jax.named_scope("combine"):
        owned = combine(got_tails.reshape(-1, width), got)
    return owned[None], relation_grad


def solution(mesh):
    fine = Mesh(mesh.devices.reshape(*SIZES.values()), tuple(SIZES))
    whole = P(ALL)
    wide = P(ALL, None)
    return jax.shard_map(
        on_device,
        mesh=fine,
        in_specs=(
            wide, wide, whole, wide, whole, wide, whole, wide, wide, whole, P("y", SHARD), P(),
        ),
        out_specs=(P("y", SHARD, None), wide),
        check_vma=False,
    )
```

```python
import jax
import jax.numpy as jnp
from jax import lax
from jax.experimental import pallas as pl
from jax.experimental.pallas import tpu as pltpu
from jax.sharding import Mesh, PartitionSpec as P

CLS_DEV = 2048
CAP = 16
CAP_N = 2
SIZES = {"y": 4, "z": 8, "x": 4, "c": 2}
SHARD = ("z", "x", "c")
ALL = ("y",) + SHARD
BF = jnp.bfloat16
F32 = jnp.float32


def swap(a, axis, flip):
    return lax.ppermute(a, axis, [(i, i ^ flip) for i in range(SIZES[axis])])


def pair_keep(arrived, keep):
    keep = keep + arrived.astype(F32)
    low = lax.axis_index("y") < 2
    send = jnp.where(low, keep[1], keep[0]).astype(BF)
    return jnp.where(low, keep[0], keep[1]) + swap(send, "y", 3).astype(F32)


def column_sum(own, dtype):
    me = lax.axis_index("x")
    block = lambda flip: lax.dynamic_index_in_dim(own, me ^ flip, 1, keepdims=False)
    moved = [swap(block(flip).astype(dtype), "x", flip).astype(F32) for flip in (1, 3, 2)]
    return block(0) + moved[0] + moved[1] + moved[2]


def onehot_of(slots, count):
    return lax.broadcasted_iota(jnp.int32, (count, slots.shape[1]), 0) == slots


def eye(n):
    return lax.broadcasted_iota(jnp.int32, (n, n), 0) == lax.broadcasted_iota(jnp.int32, (n, n), 1)


def to_column(row):
    return jnp.sum(jnp.where(eye(row.shape[1]), row.astype(F32), 0.0), axis=1, keepdims=True)


def query_kernel(heads_ref, rel_ref, relations_ref, query_ref, column_ref):
    heads = heads_ref[...].astype(F32)
    rel = to_column(rel_ref[...])
    column_ref[...] = rel.astype(jnp.int32)
    total = jnp.zeros(heads.shape, F32)
    for r in range(relations_ref.shape[0]):
        masked = jnp.where(rel == r, heads, 0.0).astype(BF)
        total += jnp.dot(masked, relations_ref[r], preferred_element_type=F32)
    query_ref[...] = total.astype(BF)


def make_query(heads, rel_id, relations):
    n = heads.shape[0]
    return pl.pallas_call(
        query_kernel,
        out_shape=(jax.ShapeDtypeStruct(heads.shape, BF), jax.ShapeDtypeStruct((n, 1), jnp.int32)),
        compiler_params=pltpu.CompilerParams(vmem_limit_bytes=32 * 2**20),
        cost_estimate=pl.CostEstimate(flops=4 * 10**9, bytes_accessed=4 * 2**20, transcendentals=0),
        name="query",
    )(heads, rel_id.reshape(1, n), relations)


FIELDS = dict(head_hi=0, tail_hi=16, neg_hi=32, head_lo=34, tail_lo=50, neg_lo=66, gpos_hi=68, gpos_lo=84)


def slots_kernel(ho_ref, to_ref, no_ref, hr_ref, tr_ref, nr_ref, hs_ref, ts_ref, ns_ref, line_ref, rank_ref):
    owners = line_ref.shape[0]
    line = jnp.zeros((owners, 128), F32)
    kinds = (("head", CAP, ho_ref, hr_ref, hs_ref), ("tail", CAP, to_ref, tr_ref, ts_ref), ("neg", CAP_N, no_ref, nr_ref, ns_ref))
    for kind, cap, owner_ref, row_ref, slots_ref in kinds:
        column = owner_ref[...].astype(F32)
        n = column.shape[0]
        row = jnp.sum(jnp.where(eye(n), column, 0.0), axis=0, keepdims=True)
        down = lax.broadcasted_iota(jnp.int32, (n, n), 0)
        across = lax.broadcasted_iota(jnp.int32, (n, n), 1)
        same = column == row
        rank_row = jnp.sum(jnp.where(same & (down < across), 1.0, 0.0), axis=0, keepdims=True)
        rank = jnp.sum(jnp.where(same & (across < down), 1.0, 0.0), axis=1, keepdims=True).astype(jnp.int32)
        slots_ref[...] = (row * cap + rank_row).astype(jnp.int32)
        if kind == "tail":
            rank_ref[...] = rank
        value = to_column(row_ref[...]).astype(jnp.int32) + 1
        field = lax.broadcasted_iota(jnp.int32, (n, 128), 1)
        put = jnp.where(field == FIELDS[kind + "_hi"] + rank, (value >> 7).astype(F32), 0.0)
        put += jnp.where(field == FIELDS[kind + "_lo"] + rank, (value & 127).astype(F32), 0.0)
        hot = lax.broadcasted_iota(jnp.int32, (owners, n), 0) == row.astype(jnp.int32)
        line += jnp.dot(jnp.where(hot, 1.0, 0.0).astype(BF), put.astype(BF), preferred_element_type=F32)
    wide = jnp.broadcast_to(line[:, None, :], (owners, 8, 128))
    line_ref[...] = jnp.where(lax.broadcasted_iota(jnp.int32, wide.shape, 1) == 0, wide, 0.0).astype(BF)


def make_slots(columns, rows, owners):
    return pl.pallas_call(
        slots_kernel,
        out_shape=tuple(jax.ShapeDtypeStruct((1, c.shape[0]), jnp.int32) for c in columns)
        + (jax.ShapeDtypeStruct((owners, 8, 128), BF), jax.ShapeDtypeStruct(columns[1].shape, jnp.int32)),
        compiler_params=pltpu.CompilerParams(vmem_limit_bytes=32 * 2**20),
        cost_estimate=pl.CostEstimate(flops=4 * 10**9, bytes_accessed=2**20, transcendentals=0),
        name="slots",
    )(*columns, *[r.reshape(1, -1) for r in rows])


def weights_kernel(count_ref, query_ref, tail_ref, near_ref, far_ref, dquery_ref, gpos_ref, own_ref, other_ref):
    query, near, far = query_ref[...], near_ref[...], far_ref[...]
    tails = tail_ref[...].astype(F32)
    n = query.shape[0]
    scores = lambda negatives: lax.dot_general(query, negatives, (((1,), (1,)), ((), ())), preferred_element_type=F32)
    near_scores, far_scores = scores(near), scores(far)
    positive = jnp.sum(query.astype(F32) * tails, axis=1, keepdims=True)
    top = jnp.maximum(jnp.max(near_scores, axis=1, keepdims=True), jnp.max(far_scores, axis=1, keepdims=True))
    top = jnp.maximum(positive, top)
    pos_exp = jnp.exp(positive - top)
    near_exp, far_exp = jnp.exp(near_scores - top), jnp.exp(far_scores - top)
    total = pos_exp + jnp.sum(near_exp, axis=1, keepdims=True) + jnp.sum(far_exp, axis=1, keepdims=True)
    live = lax.broadcasted_iota(jnp.int32, (n, 1), 0) < count_ref[0, 0]
    gpos = jnp.where(live, pos_exp / total - 1.0, 0.0)
    share = jnp.where(live, 1.0 / total, 0.0)
    near_w, far_w = (near_exp * share).astype(BF), (far_exp * share).astype(BF)
    terms = lambda w: lax.dot_general(w, query, (((0,), (0,)), ((), ())), preferred_element_type=F32)
    other_ref[...] = terms(far_w).astype(BF)
    own_ref[...] = terms(near_w)
    dquery = gpos * tails + jnp.dot(near_w, near, preferred_element_type=F32)
    dquery_ref[...] = (dquery + jnp.dot(far_w, far, preferred_element_type=F32)).astype(BF)
    gpos_ref[...] = gpos


def weights(counts, query, tails, near, far):
    n, width = query.shape
    shape = lambda rows, dtype: jax.ShapeDtypeStruct((rows, width), dtype)
    m = near.shape[0]
    return pl.pallas_call(
        weights_kernel,
        in_specs=[pl.BlockSpec(memory_space=pltpu.SMEM)] + [pl.BlockSpec(memory_space=pltpu.VMEM)] * 4,
        out_shape=(shape(n, BF), jax.ShapeDtypeStruct((n, 1), F32), shape(m, F32), shape(m, BF)),
        compiler_params=pltpu.CompilerParams(vmem_limit_bytes=40 * 2**20),
        name="weights",
    )(counts, query, tails, near, far)


NEGS, LINE, SUB = 4 * CAP, 4 * CAP + 8, 4 * CAP + 16


def tails_kernel(query_ref, slots_ref, out_ref):
    hot = jnp.where(onehot_of(slots_ref[...], out_ref.shape[0]), 1.0, 0.0).astype(BF)
    out_ref[...] = jnp.dot(hot, query_ref[...], preferred_element_type=F32).astype(BF)


def pack_tails(query, slots, owners):
    return pl.pallas_call(
        tails_kernel,
        out_shape=jax.ShapeDtypeStruct((owners * CAP, query.shape[1]), BF),
        compiler_params=pltpu.CompilerParams(vmem_limit_bytes=32 * 2**20),
        cost_estimate=pl.CostEstimate(flops=10**9, bytes_accessed=2**20, transcendentals=0),
        name="pack_tails",
    )(query, slots)


def heads_kernel(dquery_ref, rel_ref, relations_ref, slots_ref, line_ref, gpos_ref, rank_ref, tail_slots_ref, out_ref):
    owners = out_ref.shape[0]
    dquery = dquery_ref[...].astype(F32)
    n = dquery.shape[0]
    dhead = jnp.zeros(dquery.shape, F32)
    for r in range(relations_ref.shape[0]):
        masked = jnp.where(rel_ref[...] == r, dquery, 0.0).astype(BF)
        dhead += lax.dot_general(masked, relations_ref[r], (((1,), (1,)), ((), ())), preferred_element_type=F32)
    hot = jnp.where(onehot_of(slots_ref[...], owners * CAP), 1.0, 0.0).astype(BF)
    rows = jnp.dot(hot, dhead.astype(BF), preferred_element_type=F32).astype(BF)
    for block in range(4):
        at = block * CAP
        out_ref[:, at:at + CAP, :] = rows[:, block * 128:(block + 1) * 128].reshape(owners, CAP, 128)
    gpos = gpos_ref[...]
    high = gpos.astype(BF).astype(F32)
    field = lax.broadcasted_iota(jnp.int32, (n, 128), 1)
    put = jnp.where(field == FIELDS["gpos_hi"] + rank_ref[...], high, 0.0)
    put += jnp.where(field == FIELDS["gpos_lo"] + rank_ref[...], gpos - high, 0.0)
    of_owner = lax.broadcasted_iota(jnp.int32, (owners, n), 0) == tail_slots_ref[...] // CAP
    extra = jnp.dot(jnp.where(of_owner, 1.0, 0.0).astype(BF), put.astype(BF), preferred_element_type=F32)
    wide = jnp.broadcast_to(extra[:, None, :], (owners, 8, 128))
    wide = jnp.where(lax.broadcasted_iota(jnp.int32, wide.shape, 1) == 0, wide, 0.0)
    line = (line_ref[...].astype(F32) + wide).astype(BF)
    out_ref[:, NEGS:, :] = jnp.concatenate([jnp.zeros((owners, 8, 128), F32), line.astype(F32)], axis=1).astype(BF)


def pack_heads(dquery, rel_id, relations, slots, line, gpos, rank, tail_slots):
    return pl.pallas_call(
        heads_kernel,
        out_shape=jax.ShapeDtypeStruct((line.shape[0], SUB, 128), BF),
        compiler_params=pltpu.CompilerParams(vmem_limit_bytes=40 * 2**20),
        name="pack_heads",
    )(dquery, rel_id, relations, slots, line, gpos, rank, tail_slots)


def negs_kernel(terms_ref, slots_ref, have_ref, out_ref):
    owners = out_ref.shape[0]
    grad = jnp.sum(terms_ref[...].astype(F32), axis=0).astype(BF)
    entry = lax.broadcasted_iota(jnp.int32, (owners * 8, grad.shape[0]), 0)
    filled = (entry // 8) * CAP_N + entry % CAP_N == slots_ref[...]
    column = (entry % 8) // CAP_N
    rows = jnp.zeros((owners * 8, 128), F32)
    for block in range(4):
        hot = jnp.where(filled & (column == block), 1.0, 0.0).astype(BF)
        rows += jnp.dot(hot, grad[:, block * 128:(block + 1) * 128], preferred_element_type=F32)
    out_ref[...] = rows.reshape(owners, 8, 128).astype(BF)


def pack_negs(terms, slots, have):
    return pl.pallas_call(
        negs_kernel,
        grid=(1,),
        in_specs=[
            pl.BlockSpec(terms.shape, lambda i: (0, 0, 0)),
            pl.BlockSpec(slots.shape, lambda i: (0, 0)),
            pl.BlockSpec(memory_space=pl.ANY),
        ],
        out_specs=pl.BlockSpec((have.shape[0], 8, 128), lambda i: (0, NEGS // 8, 0)),
        out_shape=jax.ShapeDtypeStruct(have.shape, BF),
        input_output_aliases={2: 0},
        name="pack_negs",
    )(terms, slots, have)


def relation_kernel(inner_ref, both_ref, rel_ref, far_rel_ref, dquery_ref, far_ref, send_ref, keep_ref):
    n = dquery_ref.shape[0]
    near_rel, far_rel = rel_ref[...], to_column(far_rel_ref[...]).astype(jnp.int32)
    near_dquery, far_dquery = dquery_ref[...], far_ref[...]
    inner = inner_ref[0, 0] == 1

    def terms(relation):
        def part(rel, heads, dquery):
            masked = jnp.where(rel == relation, heads.astype(F32), 0.0).astype(BF)
            return lax.dot_general(masked, dquery, (((0,), (0,)), ((), ())), preferred_element_type=F32)

        return part(near_rel, both_ref[:n, :], near_dquery) + part(far_rel, both_ref[n:, :], far_dquery)

    for at, (outer_one, inner_one) in enumerate(((0, 1), (3, 2))):
        outer_terms, inner_terms = terms(outer_one), terms(inner_one)
        send_ref[at] = jnp.where(inner, outer_terms, inner_terms).astype(BF)
        keep_ref[at] = jnp.where(inner, inner_terms, outer_terms)


def relation_terms(inner, both, rel, far_rel, dquery, far_dquery):
    shape = (2, both.shape[1], dquery.shape[1])
    return pl.pallas_call(
        relation_kernel,
        in_specs=[pl.BlockSpec(memory_space=pltpu.SMEM)] + [pl.BlockSpec(memory_space=pltpu.VMEM)] * 5,
        out_shape=(jax.ShapeDtypeStruct(shape, BF), jax.ShapeDtypeStruct(shape, F32)),
        compiler_params=pltpu.CompilerParams(vmem_limit_bytes=40 * 2**20),
        name="relation_terms",
    )(inner, both, rel, far_rel, dquery, far_dquery)


def spread_line(block, high, low, scale, cap):
    owners = block.shape[0]
    line = block.astype(F32)[:, 0, :].astype(BF)
    total = owners * cap
    field = lax.broadcasted_iota(jnp.int32, (128, total), 0)
    place = lax.broadcasted_iota(jnp.int32, (128, total), 1) % cap
    take = jnp.where(field == FIELDS[high] + place, scale, 0.0)
    take += jnp.where(field == FIELDS[low] + place, 1.0, 0.0)
    every = jnp.dot(line, take.astype(BF), preferred_element_type=F32)
    mine = lax.broadcasted_iota(jnp.int32, (owners, total), 1) // cap
    mine = mine == lax.broadcasted_iota(jnp.int32, (owners, total), 0)
    return jnp.sum(jnp.where(mine, every, 0.0), axis=0, keepdims=True)


def combine_kernel(tails_ref, got_ref, out_ref, rows_of, ids, weights_of):
    owners = got_ref.shape[0]
    slots, negs = owners * CAP, owners * CAP_N
    rows = out_ref.shape[0]

    @pl.when(pl.program_id(0) == 0)
    def _():
        for block in range(4):
            at = block * CAP
            rows_of[:slots, block * 128:(block + 1) * 128] = got_ref[:, at:at + CAP, :].reshape(slots, 128)
        packed = got_ref[:, NEGS:LINE, :].reshape(owners * 8, 128)
        entry = lax.broadcasted_iota(jnp.int32, (negs, owners * 8), 0)
        source = lax.broadcasted_iota(jnp.int32, (negs, owners * 8), 1)
        for block in range(4):
            take = jnp.where(source == entry // CAP_N * 8 + block * CAP_N + entry % CAP_N, 1.0, 0.0).astype(BF)
            rows_of[slots:, block * 128:(block + 1) * 128] = jnp.dot(take, packed, preferred_element_type=F32).astype(BF)
        line = got_ref[:, LINE:, :]
        for first, kind, cap in ((0, "head", CAP), (slots, "neg", CAP_N), (slots + negs, "tail", CAP)):
            row = spread_line(line, kind + "_hi", kind + "_lo", 128.0, cap)
            ids[:, first:first + owners * cap] = row.astype(jnp.int32) - 1
        weights_of[...] = spread_line(line, "gpos_hi", "gpos_lo", 1.0, CAP)

    first = pl.program_id(0) * rows
    labels = ids[...]
    here = (labels >= first) & (labels < first + rows)
    here = jnp.where(here, labels - first, -1).astype(F32).astype(BF)
    cut = slots + negs

    def hot(labels, weights):
        place = lax.broadcasted_iota(jnp.int32, (rows, labels.shape[1]), 0).astype(F32).astype(BF)
        return jnp.where(place == labels, weights, jnp.zeros((1, 1), BF))

    total = jnp.dot(hot(here[:, :cut], jnp.ones((1, 1), BF)), rows_of[...], preferred_element_type=F32)
    total += jnp.dot(hot(here[:, cut:], weights_of[...].astype(BF)), tails_ref[...], preferred_element_type=F32)
    out_ref[...] = total


def combine(tails, got):
    tile, width = 256, tails.shape[1]
    slots, negs = got.shape[0] * CAP, got.shape[0] * CAP_N
    return pl.pallas_call(
        combine_kernel,
        grid=(CLS_DEV // tile,),
        in_specs=[pl.BlockSpec(tails.shape, lambda i: (0, 0)), pl.BlockSpec(got.shape, lambda i: (0, 0, 0))],
        out_specs=pl.BlockSpec((tile, width), lambda i: (i, 0)),
        out_shape=jax.ShapeDtypeStruct((CLS_DEV, width), F32),
        scratch_shapes=[
            pltpu.VMEM((slots + negs, width), BF),
            pltpu.VMEM((1, 2 * slots + negs), jnp.int32),
            pltpu.VMEM((1, slots), F32),
        ],
        compiler_params=pltpu.CompilerParams(vmem_limit_bytes=40 * 2**20),
        cost_estimate=pl.CostEstimate(flops=8 * 10**9, bytes_accessed=8 * 2**20, transcendentals=0),
        name="combine",
    )(tails, got)


def on_device(
    head_vecs, tail_vecs, rel_id, head_owner, head_row, tail_owner, tail_row,
    neg_vecs, neg_owner, neg_row, counts, relations,
):
    n, width = head_vecs.shape
    rels = relations.shape[0]
    owners = SIZES["z"] * SIZES["x"] * SIZES["c"]
    core = lax.axis_index("c")

    with jax.named_scope("query"):
        query, rel_column = make_query(head_vecs, rel_id, relations)
    with jax.named_scope("slots"):
        *slots, line, tail_rank = make_slots(
            (head_owner, tail_owner, neg_owner), (head_row, tail_row, neg_row), owners
        )
    with jax.named_scope("gather_negatives"):
        wide = jnp.broadcast_to(neg_vecs[None], (SIZES["z"],) + neg_vecs.shape)
        column = lax.all_to_all(wide, "z", 0, 0, tiled=True).reshape(-1, width)
        tail_rows = pack_tails(query, slots[1], owners)
        near = jnp.concatenate([column] + [swap(column, "x", flip) for flip in (1, 3, 2)], axis=0)
        near, tail_rows = lax.optimization_barrier((near, tail_rows))
        far = swap(near, "c", 1)
    with jax.named_scope("send_tails"):
        got_tails = lax.all_to_all(tail_rows.reshape(owners, CAP, width), SHARD, 0, 0, tiled=True)
    with jax.named_scope("rel_heads"):
        feature = lax.broadcasted_iota(jnp.int32, (width, width // 2), 0)
        place = lax.broadcasted_iota(jnp.int32, (width, width // 2), 1)
        wanted = (feature == place // 8 * 16 + core * 8 + place % 8).astype(BF)
        both = jnp.concatenate([head_vecs, swap(head_vecs, "c", 1)], axis=0)
        both = jnp.dot(both, wanted, preferred_element_type=F32).astype(BF)
        far_rel = swap(rel_id, "c", 1).reshape(1, n)
        row = lax.axis_index("y")
        inner = ((row == 1) | (row == 2)).astype(jnp.int32).reshape(1, 1)

    with jax.named_scope("weights"):
        dquery, gpos, own, other = weights(counts, query, tail_vecs, near, far)
    with jax.named_scope("neg_sum"):
        own = own + swap(other, "c", 1).astype(F32)
        own = own.reshape(4, 8, -1, width)
        moved = [swap(own[at].astype(BF), "x", flip).astype(F32) for at, flip in ((1, 1), (2, 3), (3, 2))]
        own = (own[0] + moved[0] + moved[1] + moved[2]).astype(BF)
    with jax.named_scope("pack_heads"):
        heads = pack_heads(dquery, rel_column, relations, slots[0], line, gpos, tail_rank, slots[1])
    with jax.named_scope("rel_sum"):
        mine, keep = relation_terms(inner, both, rel_column, far_rel, dquery, swap(dquery, "c", 1))
    own, got_tails, heads, mine, keep = lax.optimization_barrier((own, got_tails, heads, mine, keep))
    with jax.named_scope("neg_exchange"):
        terms = lax.all_to_all(own, "z", 0, 0, tiled=True)
    with jax.named_scope("rel_halves"):
        mine = swap(mine, "y", 1)
        terms, mine = lax.optimization_barrier((terms, mine))
    with jax.named_scope("send_heads"):
        got = lax.all_to_all(pack_negs(terms, slots[2], heads), SHARD, 0, 0, tiled=True)
    with jax.named_scope("rel_column"):
        mine = column_sum(pair_keep(mine, keep).reshape(8, 4, 8, width), F32)
        mine, got = lax.optimization_barrier((mine, got))
    with jax.named_scope("rel_end"):
        relation_grad = jnp.sum(lax.all_to_all(mine, "z", 0, 0, tiled=True), axis=0)
    with jax.named_scope("combine"):
        owned = combine(got_tails.reshape(-1, width), got)
    return owned[None], relation_grad


def solution(mesh):
    fine = Mesh(mesh.devices.reshape(*SIZES.values()), tuple(SIZES))
    whole = P(ALL)
    wide = P(ALL, None)
    return jax.shard_map(
        on_device,
        mesh=fine,
        in_specs=(
            wide, wide, whole, wide, whole, wide, whole, wide, wide, whole, P("y", SHARD), P(),
        ),
        out_specs=(P("y", SHARD, None), wide),
        check_vma=False,
    )
```
